32 devices in a mesh: dp: 2 (over core), ctx: 8 (over z, y), tp: 2 (over x).
Axes of the slice: x: 2, y: 2, z: 4, core: 2. Of those that a mesh axis runs over, the one named last changes fastest.
Arguments:
- doc_lengths: int32 [2, 4], P('dp'), may hold values from 1 to 512, 1024 in all within a row
- piece_plan: int32 [2, 16], P('dp'), may hold values from 0 to 15, each once within a row
- queries: bfloat16 [2, 1024, 8192], P('dp', 'ctx', 'tp'), may hold values from -8 to 8
- rotated_keys: bfloat16 [2, 1024, 1024], P('dp', 'ctx', 'tp'), may hold values from -8 to 8
- value_matrix: bfloat16 [2, 1024, 1024], P('dp', 'ctx', 'tp'), may hold values from -6 to 6
- output_gradient: bfloat16 [2, 1024, 8192], P('dp', 'ctx', 'tp'), may hold values from -6 to 6
- attention_output: bfloat16 [2, 1024, 8192], P('dp', 'ctx', 'tp'), may hold values from -3 to 3
- value_projection_weight: bfloat16 [8192, 1024], P('dp', 'tp'), may hold values from -0.1875 to 0.1875
Outputs:
- query_grad: bfloat16 [2, 1024, 8192], P('dp', 'ctx', 'tp')
- key_gradient: bfloat16 [2, 1024, 1024], P('dp', 'ctx', 'tp')
- value_gradient: bfloat16 [2, 1024, 1024], P('dp', 'ctx', 'tp')
- input_grad: bfloat16 [2, 1024, 8192], P('dp', 'ctx', 'tp')
The draws below stay inside these ranges and needn't reach their ends.
Inputs may be any that keep to these rules, and one draw needn't show every extreme that they name: `doc_lengths`: the 4 lengths of a micro-batch sum to 1024, and the longest is exactly half of 1024. `piece_plan`: each row names every stream piece of 64 tokens once.
All inputs are finite; a program needn't handle non-finite values.
Results may differ from the reference program's by a relative error of at most 0.012.
Values may be sent and summed in bfloat16 or wider, within the bound.
A program may use at most 128 MiB of HBM per device.

```python
import math
import jax
import jax.numpy as jnp
import numpy as np
from jax import lax

MODEL_WIDTH = 8192
QUERY_HEADS = 64
KEY_VALUE_HEADS = 8
HEAD_SIZE = 128
TOK_DEV = 128
PIECE = 64
DOCS = 4
MICRO_BATCHES = 2
BATCH_TOKENS = 1024
PIECES = 16
N_DP = 2
N_CTX = 8
N_TP = 2


def draw_queries(key, part):
    key = jax.random.fold_in(key, 21)
    return jnp.clip(jax.random.normal(key, (MICRO_BATCHES, BATCH_TOKENS, QUERY_HEADS * HEAD_SIZE), jnp.float32), -6.0, 6.0).astype(jnp.bfloat16)


def draw_rotated_keys(key, part):
    key = jax.random.fold_in(key, 22)
    return jnp.clip(jax.random.normal(key, (MICRO_BATCHES, BATCH_TOKENS, KEY_VALUE_HEADS * HEAD_SIZE), jnp.float32), -6.0, 6.0).astype(jnp.bfloat16)


def steps_of(rng, extent, cuts, least, top_value):
    gain = 1.0
    for axis_at, parts in cuts:
        draws = jax.random.uniform(jax.random.fold_in(jax.random.fold_in(rng, 6), axis_at), (parts,), jnp.float32, least / len(cuts), top_value / len(cuts))
        gain = gain * jnp.repeat(jnp.exp(draws), extent[axis_at] // parts).reshape((-1,) + (1,) * (len(extent) - 1 - axis_at))
    return gain


def split_up(amount, total, bound, slope):
    portions = [(1 << 20) // math.isqrt(grade ** slope) + 1 for grade in range(2, amount + 1)]
    spare, counts = total - bound - (amount - 1), [1] * (amount - 1)
    while spare > 0:
        free = [i for i in range(amount - 1) if counts[i] < bound]
        mass, left = sum([portions[i] for i in free]), spare
        for i in free:
            addition = min(bound - counts[i], max(1, left * portions[i] // mass), spare)
            counts[i] = counts[i] + addition
            spare = spare - addition
    return np.array([bound] + counts)


def uneven(key, amount, total, most, lean):
    if amount == 2:
        one = jax.random.randint(key, (), max(1, total - most), min(most, total - 1) + 1)
        return jnp.stack([one, total - one])
    tallies = jnp.asarray(split_up(amount, total, most, lean), jnp.int32)
    couples = (amount - 1) // 2
    giver, taker = tallies[1:1 + 2 * couples:2], tallies[2:2 + 2 * couples:2]
    room = jnp.minimum(giver - 1, most - taker)
    moved = jax.random.randint(jax.random.fold_in(key, 1), (couples,), 0, 1 << 20) % (room + 1)
    tallies = tallies.at[1:1 + 2 * couples:2].set(giver - moved).at[2:2 + 2 * couples:2].set(taker + moved)
    return tallies[jax.random.permutation(jax.random.fold_in(key, 2), amount)]


def centred(key, extent, width, limit, split=(), kind=jnp.bfloat16):
    values = width * jax.random.normal(key, extent, jnp.float32)
    if split:
        values = values * steps_of(key, extent, split, -0.22, 0.18)
    return jnp.clip(values, -limit, limit).astype(kind)


def setup_inputs(seed: int = 0) -> dict:
    seeds = jax.random.split(jax.random.key(seed), 9)
    doc_lengths = jax.vmap(lambda own: uneven(own, DOCS, BATCH_TOKENS, BATCH_TOKENS // 2, 2))(jax.random.split(seeds[0], MICRO_BATCHES)).reshape((MICRO_BATCHES, DOCS)).astype(jnp.int32)
    piece_plan = jax.vmap(lambda own: jax.random.permutation(own, PIECES))(jax.random.split(seeds[1], MICRO_BATCHES)).reshape((MICRO_BATCHES, PIECES)).astype(jnp.int32)
    queries = draw_queries(jax.random.fold_in(seeds[8], 71), 0)
    rotated_keys = draw_rotated_keys(jax.random.fold_in(seeds[8], 71), 0)
    value_matrix = centred(seeds[4], (MICRO_BATCHES, BATCH_TOKENS, KEY_VALUE_HEADS * HEAD_SIZE), 1.0, 6.0, ((0, 2), (1, 8), (2, 2)))
    output_gradient = centred(seeds[5], (MICRO_BATCHES, BATCH_TOKENS, QUERY_HEADS * HEAD_SIZE), 1.0, 6.0, ((0, 2), (1, 8), (2, 2)))
    attention_output = centred(seeds[6], (MICRO_BATCHES, BATCH_TOKENS, QUERY_HEADS * HEAD_SIZE), 0.5, 3.0, ((0, 2), (1, 8), (2, 2)))
    value_projection_weight = centred(seeds[7], (MODEL_WIDTH, KEY_VALUE_HEADS * HEAD_SIZE), (KEY_VALUE_HEADS * HEAD_SIZE) ** -0.5, 0.1875, ((0, 2), (1, 2)))
    return {"doc_lengths": doc_lengths, "piece_plan": piece_plan, "queries": queries, "rotated_keys": rotated_keys, "value_matrix": value_matrix, "output_gradient": output_gradient, "attention_output": attention_output, "value_projection_weight": value_projection_weight}


NEG = -1.0e30


def rounded(values):
    return lax.optimization_barrier(values.astype(jnp.bfloat16)).astype(jnp.float32)


def stream_layout(doc_lengths, piece_plan):
    piece_start = jnp.broadcast_to(piece_plan[:, None].astype(jnp.int32) * PIECE, (PIECES, PIECE))
    offsets = jnp.broadcast_to(jnp.arange(PIECE, dtype=jnp.int32)[None, :], (PIECES, PIECE))
    position = (piece_start + offsets).reshape(BATCH_TOKENS).astype(jnp.int32)
    doc_ends = jnp.cumsum(doc_lengths).astype(jnp.int32)
    document = jnp.sum((position[:, None] >= doc_ends[None, :]).astype(jnp.int32), axis=1).astype(jnp.int32)
    return position, document


def one_batch(doc_lengths, piece_plan, queries, rotated_keys, value_matrix, output_gradient, attention_output, value_projection_weight):
    position, document = stream_layout(doc_lengths, piece_plan)
    queries_per_group = QUERY_HEADS // KEY_VALUE_HEADS
    temper = HEAD_SIZE ** -0.5
    head_queries = queries.astype(jnp.float32).reshape(BATCH_TOKENS, KEY_VALUE_HEADS, queries_per_group, HEAD_SIZE)
    head_gradient = output_gradient.astype(jnp.float32).reshape(BATCH_TOKENS, KEY_VALUE_HEADS, queries_per_group, HEAD_SIZE)
    head_output = attention_output.astype(jnp.float32).reshape(BATCH_TOKENS, KEY_VALUE_HEADS, queries_per_group, HEAD_SIZE)
    head_keys = rotated_keys.astype(jnp.float32).reshape(BATCH_TOKENS, KEY_VALUE_HEADS, HEAD_SIZE)
    head_values = value_matrix.astype(jnp.float32).reshape(BATCH_TOKENS, KEY_VALUE_HEADS, HEAD_SIZE)
    row_delta = jnp.sum(head_gradient * head_output, axis=-1)

    def one_block(carried, shard_index):
        first_row = (shard_index * TOK_DEV).astype(jnp.int32)
        query_block = lax.dynamic_slice_in_dim(head_queries, first_row, TOK_DEV, 0)
        grad_block = lax.dynamic_slice_in_dim(head_gradient, first_row, TOK_DEV, 0)
        delta_block = lax.dynamic_slice_in_dim(row_delta, first_row, TOK_DEV, 0).transpose(1, 2, 0)
        query_pos = lax.dynamic_slice_in_dim(position, first_row, TOK_DEV, 0)
        query_doc = lax.dynamic_slice_in_dim(document, first_row, TOK_DEV, 0)
        allowed = (query_doc[:, None] == document[None, :]) & (query_pos[:, None] >= position[None, :])
        scores = jnp.einsum("tkgd,skd->kgts", query_block, head_keys) * temper
        masked = jnp.where(allowed, scores, NEG)
        row_max = jnp.max(masked, axis=-1, keepdims=True)
        row_sum = jnp.sum(jnp.where(allowed, jnp.exp(masked - row_max), 0.0), axis=-1, keepdims=True)
        log_norm = row_max + jnp.log(row_sum)
        weights = jnp.exp(jnp.where(allowed, scores - log_norm, NEG))
        weights_low = rounded(weights)
        grad_weights = jnp.einsum("tkgd,skd->kgts", grad_block, head_values)
        grad_scores = rounded(weights * (grad_weights - delta_block[..., None]) * temper)
        block_query = jnp.einsum("kgts,skd->tkgd", grad_scores, head_keys).astype(jnp.bfloat16)
        key_part = rounded(jnp.einsum("kgts,tkgd->skd", grad_scores, query_block))
        value_part = rounded(jnp.einsum("kgts,tkgd->skd", weights_low, grad_block))
        return (carried[0] + key_part, carried[1] + value_part), block_query

    initial_sums = (jnp.zeros((BATCH_TOKENS, KEY_VALUE_HEADS, HEAD_SIZE), jnp.float32), jnp.zeros((BATCH_TOKENS, KEY_VALUE_HEADS, HEAD_SIZE), jnp.float32))
    running_sums, query_blocks = lax.scan(one_block, initial_sums, jnp.arange(N_CTX, dtype=jnp.int32))
    query_grad = query_blocks.reshape(BATCH_TOKENS, QUERY_HEADS * HEAD_SIZE)
    key_gradient = running_sums[0].astype(jnp.bfloat16).reshape(BATCH_TOKENS, KEY_VALUE_HEADS * HEAD_SIZE)
    value_gradient = running_sums[1].astype(jnp.bfloat16).reshape(BATCH_TOKENS, KEY_VALUE_HEADS * HEAD_SIZE)
    column_span = KEY_VALUE_HEADS // N_TP * HEAD_SIZE
    total_grad = jnp.zeros((BATCH_TOKENS, MODEL_WIDTH), jnp.float32)
    for shard_index in range(N_TP):
        low_col = shard_index * column_span
        partial_value = jnp.dot(value_gradient[:, low_col:low_col + column_span], value_projection_weight[:, low_col:low_col + column_span].T, preferred_element_type=jnp.float32)
        total_grad = total_grad + rounded(partial_value)
    return query_grad, key_gradient, value_gradient, total_grad.astype(jnp.bfloat16)


def reference(doc_lengths, piece_plan, queries, rotated_keys, value_matrix, output_gradient, attention_output, value_projection_weight):
    results = [one_batch(doc_lengths[batch], piece_plan[batch], queries[batch], rotated_keys[batch], value_matrix[batch], output_gradient[batch], attention_output[batch], value_projection_weight) for batch in range(N_DP)]
    return (jnp.stack([entry[0] for entry in results]), jnp.stack([entry[1] for entry in results]), jnp.stack([entry[2] for entry in results]), jnp.stack([entry[3] for entry in results]))
```

```python
import functools
import math

import jax
import jax.numpy as jnp
from jax import lax
from jax.experimental import pallas as pl
from jax.experimental.pallas import tpu as pltpu
from jax.sharding import PartitionSpec as P

QUERY_HEADS = 64
KEY_VALUE_HEADS = 8
HEAD_SIZE = 128
PIECE = 64
NEG = -1e30
MESH = pl.DeviceIdType.MESH
NT = (((1,), (1,)), ((), ()))
TN = (((0,), (0,)), ((), ()))
VMEM_LIMIT = 56 * 1024 * 1024


def ring_place(index, n):
    odd = index % 2
    return (1 - odd) * (index // 2) + odd * (n - 1 - index // 2)


def ring_member(place, n):
    back = place // (n // 2)
    return (1 - back) * (2 * place) + back * (2 * (n - place) - 1)


def around(n):
    me = lax.axis_index("ctx")
    place = ring_place(me, n)

    def member(offset):
        return ring_member((place + offset + 2 * n) % n, n)

    return me, member


def gather_kernel(n, k_ref, v_ref, k_all, v_all, send_sem, recv_sem, own_sem):
    me, member = around(n)
    right, left = member(1), member(-1)
    barrier = pltpu.get_barrier_semaphore()
    for peer in (left, right):
        pl.semaphore_signal(barrier, inc=1, device_id={"ctx": peer}, device_id_type=MESH)
    own = [
        pltpu.make_async_copy(k_ref, k_all.at[me], own_sem.at[0]),
        pltpu.make_async_copy(v_ref, v_all.at[me], own_sem.at[1]),
    ]
    for copy in own:
        copy.start()
    pl.semaphore_wait(barrier, 2)
    long, short = n // 2, (n - 1) // 2
    streams = []
    for tensor, (source, target) in enumerate(((k_ref, k_all), (v_ref, v_all))):
        streams.append((source, target, 1, long if tensor == 0 else short, 2 * tensor))
        streams.append((source, target, -1, short if tensor == 0 else long, 2 * tensor + 1))
    copies = {}
    for step in range(long):
        for source, target, way, count, row in streams:
            if step >= count:
                continue
            block = member(-way * step)
            if step > 0:
                copies[row, step - 1].wait_recv()
            copy = pltpu.make_async_remote_copy(
                src_ref=source if step == 0 else target.at[block],
                dst_ref=target.at[block],
                send_sem=send_sem.at[row, step],
                recv_sem=recv_sem.at[row, step],
                device_id={"ctx": right if way == 1 else left},
                device_id_type=MESH,
            )
            copy.start()
            copies[row, step] = copy
    for source, target, way, count, row in streams:
        copies[row, count - 1].wait_recv()
    for copy in copies.values():
        copy.wait_send()
    for copy in own:
        copy.wait()


def gather(keys, values, n):
    rows, width = keys.shape
    whole = jax.ShapeDtypeStruct((n, rows, width), keys.dtype)
    steps = n // 2
    return pl.pallas_call(
        functools.partial(gather_kernel, n),
        out_shape=(whole, whole),
        in_specs=[pl.BlockSpec(memory_space=pl.ANY)] * 2,
        out_specs=[pl.BlockSpec(memory_space=pl.ANY)] * 2,
        scratch_shapes=[
            pltpu.SemaphoreType.DMA((4, steps)),
            pltpu.SemaphoreType.DMA((4, steps)),
            pltpu.SemaphoreType.DMA((2,)),
        ],
        compiler_params=pltpu.CompilerParams(collective_id=0, has_side_effects=True),
        name="gather_kv",
    )(keys, values)


def attention_kernel(
    pairs,
    chunk,
    lengths,
    plan,
    first_slot,
    q_ref,
    g_ref,
    o_ref,
    k_ref,
    v_ref,
    dq_ref,
    dk_ref,
    dv_ref,
    bias,
    scores,
    dk_acc,
    dv_acc,
):
    group, pair = pl.program_id(0), pl.program_id(1)
    keys, toks = bias.shape
    chunks = keys // chunk
    heads = q_ref.shape[1] // HEAD_SIZE

    @pl.when((group == 0) & (pair == 0))
    def _():
        lane = lax.broadcasted_iota(jnp.int32, (1, toks), 1)
        row_pos = jnp.zeros((1, toks), jnp.int32)
        for piece in range(toks // PIECE):
            here = plan[first_slot[0] + piece] * PIECE + lane - piece * PIECE
            row_pos = jnp.where(lane // PIECE == piece, here, row_pos)
        start = jnp.zeros((1, toks), jnp.int32)
        end = jnp.int32(0)
        for doc in range(lengths.shape[0]):
            end = end + lengths[doc]
            start = jnp.where(row_pos >= end, end, start)

        def fill(slot, carry):
            key_pos = plan[slot] * PIECE + lax.broadcasted_iota(jnp.int32, (PIECE, toks), 0)
            allowed = (key_pos >= start) & (key_pos <= row_pos)
            bias[pl.ds(pl.multiple_of(slot * PIECE, PIECE), PIECE), :] = jnp.where(allowed, 0.0, NEG)
            return carry

        lax.fori_loop(0, keys // PIECE, fill, 0)

    def stacked(ref):
        return jnp.concatenate(
            [ref[:, h * HEAD_SIZE : (h + 1) * HEAD_SIZE] for h in range(heads)], axis=0
        )

    queries, grads = stacked(q_ref), stacked(g_ref)
    product = grads.astype(jnp.float32) * stacked(o_ref).astype(jnp.float32)
    delta = jnp.sum(product.T, axis=0, keepdims=True)
    temper = HEAD_SIZE**-0.5
    scale = temper * math.log2(math.e)
    top = None
    for c in range(chunks):
        span = pl.ds(c * chunk, chunk)
        raw = lax.dot_general(k_ref[span, :], queries, NT, preferred_element_type=jnp.float32)
        block = raw * scale + jnp.concatenate([bias[span, :]] * heads, axis=1)
        scores[span, :] = block
        high = jnp.max(block.reshape(chunk // 8, 8, block.shape[1]), axis=0)
        top = high if top is None else jnp.maximum(top, high)
    top = jnp.max(top, axis=0, keepdims=True)
    total = None
    for c in range(chunks):
        span = pl.ds(c * chunk, chunk)
        block = jnp.exp2(scores[span, :] - top)
        scores[span, :] = block
        low = jnp.sum(block.reshape(chunk // 8, 8, block.shape[1]), axis=0)
        total = low if total is None else total + low
    inverse = 1.0 / jnp.sum(total, axis=0, keepdims=True)
    dq = None
    for c in range(chunks):
        span = pl.ds(c * chunk, chunk)
        weights = scores[span, :] * inverse
        grad_weights = lax.dot_general(
            v_ref[span, :], grads, NT, preferred_element_type=jnp.float32
        )
        dv = jnp.dot(weights.astype(jnp.bfloat16), grads, preferred_element_type=jnp.float32)
        grad_scores = (weights * ((grad_weights - delta) * temper)).astype(jnp.bfloat16)
        dk = jnp.dot(grad_scores, queries, preferred_element_type=jnp.float32)
        part = lax.dot_general(
            grad_scores, k_ref[span, :], TN, preferred_element_type=jnp.float32
        )
        dq = part if dq is None else dq + part

        @pl.when(pair == 0)
        def _():
            dv_acc[span, :] = dv
            dk_acc[span, :] = dk

        @pl.when(pair > 0)
        def _():
            dv_acc[span, :] += dv
            dk_acc[span, :] += dk

    for h in range(heads):
        dq_ref[:, h * HEAD_SIZE : (h + 1) * HEAD_SIZE] = dq[h * toks : (h + 1) * toks].astype(
            dq_ref.dtype
        )

    @pl.when(pair == pairs - 1)
    def _():
        dk_ref[...] = dk_acc[...].astype(dk_ref.dtype)
        dv_ref[...] = dv_acc[...].astype(dv_ref.dtype)


def attention(lengths, plan, first_slot, queries, grads, outputs, keys, values):
    toks, q_width = queries.shape
    rows, kv_width = keys.shape
    kv_heads = kv_width // HEAD_SIZE
    per_group = q_width // kv_width
    heads = 2
    pairs = per_group // heads
    chunk = 256
    wide = pl.BlockSpec((toks, heads * HEAD_SIZE), lambda g, p, *_: (0, g * pairs + p))
    tall = pl.BlockSpec((rows, HEAD_SIZE), lambda g, p, *_: (0, g))
    cols = heads * toks
    return pl.pallas_call(
        functools.partial(attention_kernel, pairs, chunk),
        grid_spec=pltpu.PrefetchScalarGridSpec(
            num_scalar_prefetch=3,
            grid=(kv_heads, pairs),
            in_specs=[wide, wide, wide, tall, tall],
            out_specs=[wide, tall, tall],
            scratch_shapes=[
                pltpu.VMEM((rows, toks), jnp.float32),
                pltpu.VMEM((rows, cols), jnp.float32),
                pltpu.VMEM((rows, HEAD_SIZE), jnp.float32),
                pltpu.VMEM((rows, HEAD_SIZE), jnp.float32),
            ],
        ),
        out_shape=(
            jax.ShapeDtypeStruct((toks, q_width), queries.dtype),
            jax.ShapeDtypeStruct((rows, kv_width), keys.dtype),
            jax.ShapeDtypeStruct((rows, kv_width), keys.dtype),
        ),
        compiler_params=pltpu.CompilerParams(vmem_limit_bytes=VMEM_LIMIT),
        name="attention_backward",
    )(lengths, plan, first_slot, queries, grads, outputs, keys, values)


def reduce_kernel(
    n,
    n_tp,
    chunk,
    k_part,
    v_part,
    w_ref,
    dk_ref,
    dv_ref,
    di_ref,
    weight,
    ring_send,
    ring_recv,
    part_send,
    part_recv,
    ring_send_sem,
    ring_recv_sem,
    part_send_sem,
    part_recv_sem,
    w_sem,
):
    me, member = around(n)
    dp, tp = lax.axis_index("dp"), lax.axis_index("tp")
    other = 1 - dp
    right, left = member(1), member(-1)
    half = w_ref.shape[0]
    share = 2 * half // n_tp
    chunks = share // chunk
    barrier = pltpu.get_barrier_semaphore()
    for peer in (left, right):
        pl.semaphore_signal(barrier, inc=1, device_id={"ctx": peer}, device_id_type=MESH)
    pl.semaphore_signal(barrier, inc=1, device_id={"dp": other}, device_id_type=MESH)
    for k in range(1, n_tp):
        pl.semaphore_signal(barrier, inc=1, device_id={"tp": (tp + k) % n_tp}, device_id_type=MESH)
    own_rows = pl.ds(pl.multiple_of(dp * half, half), half)
    w_own = pltpu.make_async_copy(w_ref, weight.at[own_rows], w_sem.at[0])
    w_own.start()
    pl.semaphore_wait(barrier, 2 + n_tp)
    w_copy = pltpu.make_async_remote_copy(
        src_ref=w_ref,
        dst_ref=weight.at[own_rows],
        send_sem=w_sem.at[1],
        recv_sem=w_sem.at[2],
        device_id={"dp": other},
        device_id_type=MESH,
    )
    long, short = n // 2, (n - 1) // 2
    copies = []
    rings = {}

    def ring_step(tensor, part, way, count, step):
        row = 2 * tensor + (0 if way == 1 else 1)
        place = member(way * (count - step))
        block = part[place].astype(jnp.float32)
        if step > 0:
            rings[row, step - 1].wait_recv()
            block = block + ring_recv[row, step - 1].astype(jnp.float32)
        ring_send[row, step] = block.astype(jnp.bfloat16)
        copy = pltpu.make_async_remote_copy(
            src_ref=ring_send.at[row, step],
            dst_ref=ring_recv.at[row, step],
            send_sem=ring_send_sem.at[row, step],
            recv_sem=ring_recv_sem.at[row, step],
            device_id={"ctx": right if way == 1 else left},
            device_id_type=MESH,
        )
        copy.start()
        rings[row, step] = copy
        copies.append(copy)

    def ring_end(tensor, part, counts):
        block = part[me].astype(jnp.float32)
        for at, count in enumerate(counts):
            rings[2 * tensor + at, count - 1].wait_recv()
            block = block + ring_recv[2 * tensor + at, count - 1].astype(jnp.float32)
        return block.astype(jnp.bfloat16)

    for step in range(long):
        ring_step(1, v_part, 1, long, step)
        if step < short:
            ring_step(1, v_part, -1, short, step)
        if step == 0:
            w_copy.start()
    ring_step(0, k_part, 1, short, 0)
    ring_step(0, k_part, -1, long, 0)
    value_grad = ring_end(1, v_part, (long, short))
    dv_ref[...] = value_grad
    w_own.wait()
    w_copy.wait()

    def product(part, c):
        rows = pl.ds(pl.multiple_of(part * share + c * chunk, chunk), chunk)
        return lax.dot_general(
            value_grad, weight[rows, :], NT, preferred_element_type=jnp.float32
        ).astype(jnp.bfloat16)

    pending = list(range(1, long))

    def key_step():
        if pending:
            step = pending.pop(0)
            if step < short:
                ring_step(0, k_part, 1, short, step)
            ring_step(0, k_part, -1, long, step)

    parts = {}
    done = 0
    for c in range(chunks):
        for k in range(1, n_tp):
            peer = (tp + k) % n_tp
            part_send[k - 1, c] = product(peer, c)
            copy = pltpu.make_async_remote_copy(
                src_ref=part_send.at[k - 1, c],
                dst_ref=part_recv.at[k - 1, c],
                send_sem=part_send_sem.at[k - 1, c],
                recv_sem=part_recv_sem.at[k - 1, c],
                device_id={"tp": peer},
                device_id_type=MESH,
            )
            copy.start()
            parts[k, c] = copy
            copies.append(copy)
            done += 1
            if done % 3 == 0:
                key_step()
    while pending:
        key_step()
    for c in range(chunks):
        total = product(tp, c).astype(jnp.float32)
        for k in range(1, n_tp):
            parts[k, c].wait_recv()
            total = total + part_recv[k - 1, c].astype(jnp.float32)
        di_ref[:, c * chunk : (c + 1) * chunk] = total.astype(jnp.bfloat16)
    dk_ref[...] = ring_end(0, k_part, (short, long))
    for copy in copies:
        copy.wait_send()


def reduce(key_part, value_part, weight, n, n_tp):
    rows, width = key_part.shape[0] // n, key_part.shape[1]
    half = weight.shape[0]
    share = 2 * half // n_tp
    chunk = 512
    chunks = share // chunk
    steps = n // 2
    vmem = pl.BlockSpec(memory_space=pltpu.VMEM)
    narrow = jax.ShapeDtypeStruct((rows, width), jnp.bfloat16)
    return pl.pallas_call(
        functools.partial(reduce_kernel, n, n_tp, chunk),
        out_shape=(narrow, narrow, jax.ShapeDtypeStruct((rows, share), jnp.bfloat16)),
        in_specs=[vmem, vmem, pl.BlockSpec(memory_space=pl.ANY)],
        out_specs=[vmem] * 3,
        scratch_shapes=[
            pltpu.VMEM((2 * half, width), jnp.bfloat16),
            pltpu.VMEM((4, steps, rows, width), jnp.bfloat16),
            pltpu.VMEM((4, steps, rows, width), jnp.bfloat16),
            pltpu.VMEM((n_tp - 1, chunks, rows, chunk), jnp.bfloat16),
            pltpu.VMEM((n_tp - 1, chunks, rows, chunk), jnp.bfloat16),
            pltpu.SemaphoreType.DMA((4, steps)),
            pltpu.SemaphoreType.DMA((4, steps)),
            pltpu.SemaphoreType.DMA((n_tp - 1, chunks)),
            pltpu.SemaphoreType.DMA((n_tp - 1, chunks)),
            pltpu.SemaphoreType.DMA((3,)),
        ],
        compiler_params=pltpu.CompilerParams(
            collective_id=1, has_side_effects=True, vmem_limit_bytes=VMEM_LIMIT
        ),
        name="reduce_gradients",
    )(key_part.reshape(n, rows, width), value_part.reshape(n, rows, width), weight)


def solution(mesh):
    n, n_tp = mesh.shape["ctx"], mesh.shape["tp"]

    def on_device(lengths, plan, queries, keys, values, grads, outputs, weight):
        toks, width = keys.shape[1:]
        all_keys, all_values = gather(keys[0], values[0], n)
        first_slot = (lax.axis_index("ctx") * (toks // PIECE)).astype(jnp.int32).reshape(1)
        query_grad, key_part, value_part = attention(
            lengths[0],
            plan[0],
            first_slot,
            queries[0],
            grads[0],
            outputs[0],
            all_keys.reshape(n * toks, width),
            all_values.reshape(n * toks, width),
        )
        key_grad, value_grad, input_grad = reduce(key_part, value_part, weight, n, n_tp)
        return query_grad[None], key_grad[None], value_grad[None], input_grad[None]

    spread = P("dp", "ctx", "tp")
    return jax.shard_map(
        on_device,
        mesh=mesh,
        in_specs=(P("dp", None), P("dp", None)) + (spread,) * 5 + (P("dp", "tp"),),
        out_specs=(spread,) * 4,
        check_vma=False,
    )
```

```python
import functools
import math

import jax
import jax.numpy as jnp
from jax import lax
from jax.experimental import pallas as pl
from jax.experimental.pallas import tpu as pltpu
from jax.sharding import PartitionSpec as P

QUERY_HEADS = 64
KEY_VALUE_HEADS = 8
HEAD_SIZE = 128
PIECE = 64
NEG = -1e30
MESH = pl.DeviceIdType.MESH
NT = (((1,), (1,)), ((), ()))
TN = (((0,), (0,)), ((), ()))
VMEM_LIMIT = 56 * 1024 * 1024


def ring_place(index, n):
    odd = index % 2
    return (1 - odd) * (index // 2) + odd * (n - 1 - index // 2)


def ring_member(place, n):
    back = place // (n // 2)
    return (1 - back) * (2 * place) + back * (2 * (n - place) - 1)


def around(n):
    me = lax.axis_index("ctx")
    place = ring_place(me, n)

    def member(offset):
        return ring_member((place + offset + 2 * n) % n, n)

    return me, member


def fused_kernel(
    n,
    n_tp,
    chunk,
    lengths,
    plan,
    q_hbm,
    g_hbm,
    o_hbm,
    k_hbm,
    v_hbm,
    w_hbm,
    dq_ref,
    dk_ref,
    dv_ref,
    di_ref,
    q_wide,
    g_wide,
    o_wide,
    k_all,
    v_all,
    queries,
    grads,
    delta,
    bias,
    scores,
    top,
    inverse,
    dq_acc,
    k_part,
    v_part,
    value_grad,
    weight,
    ring_send,
    ring_recv,
    part_send,
    part_recv,
    load_sem,
    ag_send_sem,
    ag_recv_sem,
    ring_send_sem,
    ring_recv_sem,
    part_send_sem,
    part_recv_sem,
    w_sem,
):
    me, member = around(n)
    dp, tp = lax.axis_index("dp"), lax.axis_index("tp")
    other = 1 - dp
    right, left = member(1), member(-1)
    toks, kv_width = k_hbm.shape
    kv_heads = kv_width // HEAD_SIZE
    per_group = q_hbm.shape[1] // kv_width
    cols = per_group * toks
    half = w_hbm.shape[0]
    share = 2 * half // n_tp
    chunks = share // chunk
    long, short = n // 2, (n - 1) // 2
    low = jnp.bfloat16

    def aim(way):
        return {"ctx": right if way == 1 else left}

    barrier = pltpu.get_barrier_semaphore()
    for peer in (left, right):
        pl.semaphore_signal(barrier, inc=1, device_id={"ctx": peer}, device_id_type=MESH)
    pl.semaphore_signal(barrier, inc=1, device_id={"dp": other}, device_id_type=MESH)
    for k in range(1, n_tp):
        pl.semaphore_signal(barrier, inc=1, device_id={"tp": (tp + k) % n_tp}, device_id_type=MESH)
    own_rows = pl.ds(pl.multiple_of(dp * half, half), half)
    loads = [
        pltpu.make_async_copy(source, target, load_sem.at[i])
        for i, (source, target) in enumerate(
            (
                (k_hbm, k_all.at[me]),
                (q_hbm, q_wide),
                (g_hbm, g_wide),
                (o_hbm, o_wide),
                (v_hbm, v_all.at[me]),
                (w_hbm, weight.at[own_rows]),
            )
        )
    ]
    for load in loads:
        load.start()
    pl.semaphore_wait(barrier, 2 + n_tp)
    sends = []
    gathers = {}

    def gather_step(tensor, way, step):
        source, target = ((k_hbm, k_all), (v_hbm, v_all))[tensor]
        row = 2 * tensor + (0 if way == 1 else 1)
        block = member(-way * step)
        if step > 0:
            gathers[row, step - 1].wait_recv()
        count = long if (tensor == 0) == (way == 1) else short
        if step >= count:
            return
        copy = pltpu.make_async_remote_copy(
            src_ref=source if step == 0 else target.at[block],
            dst_ref=target.at[block],
            send_sem=ag_send_sem.at[row, step],
            recv_sem=ag_recv_sem.at[row, step],
            device_id=aim(way),
            device_id_type=MESH,
        )
        copy.start()
        gathers[row, step] = copy
        sends.append(copy)

    gather_step(0, 1, 0)
    gather_step(0, -1, 0)
    w_copy = pltpu.make_async_remote_copy(
        src_ref=w_hbm,
        dst_ref=weight.at[own_rows],
        send_sem=w_sem.at[0],
        recv_sem=w_sem.at[1],
        device_id={"dp": other},
        device_id_type=MESH,
    )
    w_copy.start()

    lane = lax.broadcasted_iota(jnp.int32, (1, toks), 1)
    row_pos = jnp.zeros((1, toks), jnp.int32)
    for piece in range(toks // PIECE):
        here = plan[me * (toks // PIECE) + piece] * PIECE + lane - piece * PIECE
        row_pos = jnp.where(lane // PIECE == piece, here, row_pos)
    start = jnp.zeros((1, toks), jnp.int32)
    end = jnp.int32(0)
    for doc in range(lengths.shape[0]):
        end = end + lengths[doc]
        start = jnp.where(row_pos >= end, end, start)

    def fill(slot, carry):
        key_pos = plan[slot] * PIECE + lax.broadcasted_iota(jnp.int32, (PIECE, toks), 0)
        allowed = (key_pos >= start) & (key_pos <= row_pos)
        bias[pl.ds(pl.multiple_of(slot * PIECE, PIECE), PIECE), :] = jnp.where(allowed, 0.0, NEG)
        return carry

    lax.fori_loop(0, n * toks // PIECE, fill, 0)

    def head_span(h):
        return pl.ds(h * HEAD_SIZE, HEAD_SIZE)

    scale = HEAD_SIZE**-0.5 * math.log2(math.e)

    def score_block(block, first):
        rows = pl.ds(pl.multiple_of(block * toks, toks), toks)
        mask = jnp.concatenate([bias[rows, :]] * per_group, axis=1)
        for g in range(kv_heads):
            raw = lax.dot_general(
                k_all[block, :, head_span(g)], queries[g], NT, preferred_element_type=jnp.float32
            )
            part = raw * scale + mask
            scores[g, rows, :] = part
            high = jnp.max(part.reshape(toks // 8, 8, cols), axis=0)
            top[g] = high if first else jnp.maximum(top[g], high)

    loads[1].wait()
    for g in range(kv_heads):
        for h in range(per_group):
            queries[g, h * toks : (h + 1) * toks, :] = q_wide[:, head_span(g * per_group + h)]
    loads[0].wait()
    score_block(me, True)
    loads[2].wait()
    loads[3].wait()

    def prepare(g):
        for h in range(per_group):
            span = head_span(g * per_group + h)
            grads[g, h * toks : (h + 1) * toks, :] = g_wide[:, span]
            term = g_wide[:, span].astype(jnp.float32) * o_wide[:, span].astype(jnp.float32)
            delta[g, :, h * toks : (h + 1) * toks] = jnp.sum(term.T, axis=0, keepdims=True)

    todo = list(range(kv_heads))
    for step in range(1, long + 1):
        gather_step(0, 1, step)
        if step <= short:
            gather_step(0, -1, step)
        if step >= long - 1 and step - long + 1 < long:
            gather_step(1, 1, step - long + 1)
            gather_step(1, -1, step - long + 1)
        if todo:
            prepare(todo.pop(0))
        score_block(member(-step), False)
        if step <= short:
            score_block(member(step), False)
    for g in todo:
        prepare(g)
    value_steps = list(range(2, long + 1))

    def value_gather():
        if value_steps:
            step = value_steps.pop(0)
            if step <= short:
                gather_step(1, 1, step)
            gather_step(1, -1, step)

    rings = {}

    def ring_step(tensor, g, way, count, step):
        part = v_part if tensor else k_part
        row = 2 * tensor + (0 if way == 1 else 1)
        block = part[g, member(way * (count - step))].astype(jnp.float32)
        if step > 0:
            rings[row, g, step - 1].wait_recv()
            block = block + ring_recv[row, g, step - 1].astype(jnp.float32)
        ring_send[row, g, step] = block.astype(low)
        copy = pltpu.make_async_remote_copy(
            src_ref=ring_send.at[row, g, step],
            dst_ref=ring_recv.at[row, g, step],
            send_sem=ring_send_sem.at[row, g, step],
            recv_sem=ring_recv_sem.at[row, g, step],
            device_id=aim(way),
            device_id_type=MESH,
        )
        copy.start()
        rings[row, g, step] = copy
        sends.append(copy)

    active = []

    def advance():
        for chain in list(active):
            tensor, g, step = chain
            counts = (long, short) if tensor else (short, long)
            for at, way in enumerate((1, -1)):
                if step < counts[at]:
                    ring_step(tensor, g, way, counts[at], step)
            if step == long:
                part = v_part if tensor else k_part
                block = part[g, me].astype(jnp.float32)
                for at in range(2):
                    row = 2 * tensor + at
                    rings[row, g, counts[at] - 1].wait_recv()
                    block = block + ring_recv[row, g, counts[at] - 1].astype(jnp.float32)
                block = block.astype(low)
                if tensor:
                    dv_ref[:, head_span(g)] = block
                    value_grad[:, head_span(g)] = block
                else:
                    dk_ref[:, head_span(g)] = block
                active.remove(chain)
            chain[2] += 1

    segments = 4
    per_segment = n // segments
    for g in range(kv_heads):
        high = jnp.max(top[g], axis=0, keepdims=True)

        def expo(j, total):
            rows = pl.ds(pl.multiple_of(j * toks, toks), toks)
            part = jnp.exp2(scores[g, rows, :] - high)
            scores[g, rows, :] = part
            return total + jnp.sum(part.reshape(toks // 8, 8, cols), axis=0)

        total = lax.fori_loop(0, n, expo, jnp.zeros((8, cols), jnp.float32))
        inverse[g] = 1.0 / jnp.sum(total, axis=0, keepdims=True)
        value_gather()

        def values_of(j, carry):
            rows = pl.ds(pl.multiple_of(j * toks, toks), toks)
            weights = scores[g, rows, :] * inverse[g]
            scores[g, rows, :] = weights
            v_part[g, j] = jnp.dot(
                weights.astype(low), grads[g], preferred_element_type=jnp.float32
            ).astype(low)
            return carry

        lax.fori_loop(0, n, values_of, 0)
        advance()
        active.append([1, g, 0])
    while value_steps:
        value_gather()
    if short == 0 or long == short:
        gather_step(1, 1, short)
    for load in loads[4:]:
        load.wait()
    advance()

    def product(part, c):
        rows = pl.ds(pl.multiple_of(part * share + c * chunk, chunk), chunk)
        return lax.dot_general(
            value_grad[...], weight[rows, :], NT, preferred_element_type=jnp.float32
        ).astype(low)

    parts = {}
    remaining = [(k, c) for c in range(chunks) for k in range(1, n_tp)]

    def send_part():
        if not remaining:
            return
        k, c = remaining.pop(0)
        peer = (tp + k) % n_tp
        part_send[k - 1, c] = product(peer, c)
        copy = pltpu.make_async_remote_copy(
            src_ref=part_send.at[k - 1, c],
            dst_ref=part_recv.at[k - 1, c],
            send_sem=part_send_sem.at[k - 1, c],
            recv_sem=part_recv_sem.at[k - 1, c],
            device_id={"tp": peer},
            device_id_type=MESH,
        )
        copy.start()
        parts[k, c] = copy
        sends.append(copy)

    arrived = False
    for g in range(kv_heads):
        for segment in range(segments):

            def keys_of(j, carry):
                rows = pl.ds(pl.multiple_of(j * toks, toks), toks)
                grad_weights = lax.dot_general(
                    v_all[j, :, head_span(g)], grads[g], NT, preferred_element_type=jnp.float32
                )
                grad_scores = (
                    scores[g, rows, :] * ((grad_weights - delta[g]) * HEAD_SIZE**-0.5)
                ).astype(low)
                k_part[g, j] = jnp.dot(
                    grad_scores, queries[g], preferred_element_type=jnp.float32
                ).astype(low)
                part = lax.dot_general(
                    grad_scores, k_all[j, :, head_span(g)], TN, preferred_element_type=jnp.float32
                )
                dq_acc[...] += part
                return carry

            if segment == 0:
                dq_acc[...] = jnp.zeros_like(dq_acc)
            lax.fori_loop(segment * per_segment, (segment + 1) * per_segment, keys_of, 0)
            if segment == segments - 1:
                active.append([0, g, 0])
            advance()
            if not any(chain[0] for chain in active):
                if not arrived:
                    w_copy.wait()
                    arrived = True
                send_part()
        for h in range(per_group):
            dq_ref[:, head_span(g * per_group + h)] = dq_acc[h * toks : (h + 1) * toks].astype(low)
    while any(chain[0] for chain in active):
        advance()
    if not arrived:
        w_copy.wait()
    while remaining:
        send_part()
        if len(remaining) % 2 == 0:
            advance()
    while active:
        advance()
    for c in range(chunks):
        total = product(tp, c).astype(jnp.float32)
        for k in range(1, n_tp):
            parts[k, c].wait_recv()
            total = total + part_recv[k - 1, c].astype(jnp.float32)
        di_ref[:, c * chunk : (c + 1) * chunk] = total.astype(low)
    for copy in sends:
        copy.wait_send()


def solution(mesh):
    n, n_tp = mesh.shape["ctx"], mesh.shape["tp"]

    def on_device(lengths, plan, queries, keys, values, grads, outputs, weight):
        toks, kv_width = keys.shape[1:]
        q_width = queries.shape[2]
        kv_heads = kv_width // HEAD_SIZE
        cols = q_width // kv_width * toks
        half = weight.shape[0]
        share = 2 * half // n_tp
        chunk = 512
        chunks = share // chunk
        steps = n // 2
        low, wide = jnp.bfloat16, jnp.float32
        vmem = pl.BlockSpec(memory_space=pltpu.VMEM)
        smem = pl.BlockSpec(memory_space=pltpu.SMEM)
        hbm = pl.BlockSpec(memory_space=pl.ANY)
        narrow = jax.ShapeDtypeStruct((toks, kv_width), low)
        dma = pltpu.SemaphoreType.DMA
        query_grad, key_grad, value_grad, input_grad = pl.pallas_call(
            functools.partial(fused_kernel, n, n_tp, chunk),
            out_shape=(
                jax.ShapeDtypeStruct((toks, q_width), low),
                narrow,
                narrow,
                jax.ShapeDtypeStruct((toks, share), low),
            ),
            in_specs=[smem] * 2 + [hbm] * 6,
            out_specs=[vmem] * 4,
            scratch_shapes=[
                pltpu.VMEM((toks, q_width), low),
                pltpu.VMEM((toks, q_width), low),
                pltpu.VMEM((toks, q_width), low),
                pltpu.VMEM((n, toks, kv_width), low),
                pltpu.VMEM((n, toks, kv_width), low),
                pltpu.VMEM((kv_heads, cols, HEAD_SIZE), low),
                pltpu.VMEM((kv_heads, cols, HEAD_SIZE), low),
                pltpu.VMEM((kv_heads, 1, cols), wide),
                pltpu.VMEM((n * toks, toks), wide),
                pltpu.VMEM((kv_heads, n * toks, cols), wide),
                pltpu.VMEM((kv_heads, 8, cols), wide),
                pltpu.VMEM((kv_heads, 1, cols), wide),
                pltpu.VMEM((cols, HEAD_SIZE), wide),
                pltpu.VMEM((kv_heads, n, toks, HEAD_SIZE), low),
                pltpu.VMEM((kv_heads, n, toks, HEAD_SIZE), low),
                pltpu.VMEM((toks, kv_width), low),
                pltpu.VMEM((2 * half, kv_width), low),
                pltpu.VMEM((4, kv_heads, steps, toks, HEAD_SIZE), low),
                pltpu.VMEM((4, kv_heads, steps, toks, HEAD_SIZE), low),
                pltpu.VMEM((n_tp - 1, chunks, toks, chunk), low),
                pltpu.VMEM((n_tp - 1, chunks, toks, chunk), low),
                dma((6,)),
                dma((4, steps)),
                dma((4, steps)),
                dma((4, kv_heads, steps)),
                dma((4, kv_heads, steps)),
                dma((n_tp - 1, chunks)),
                dma((n_tp - 1, chunks)),
                dma((2,)),
            ],
            compiler_params=pltpu.CompilerParams(
                collective_id=0, has_side_effects=True, vmem_limit_bytes=VMEM_LIMIT
            ),
            name="fused_backward",
        )(lengths[0], plan[0], queries[0], grads[0], outputs[0], keys[0], values[0], weight)
        return query_grad[None], key_grad[None], value_grad[None], input_grad[None]

    spread = P("dp", "ctx", "tp")
    return jax.shard_map(
        on_device,
        mesh=mesh,
        in_specs=(P("dp", None), P("dp", None)) + (spread,) * 5 + (P("dp", "tp"),),
        out_specs=(spread,) * 4,
        check_vma=False,
    )
```

```python
import functools
import math

import jax
import jax.numpy as jnp
from jax import lax
from jax.experimental import pallas as pl
from jax.experimental.pallas import tpu as pltpu
from jax.sharding import PartitionSpec as P

QUERY_HEADS = 64
KEY_VALUE_HEADS = 8
HEAD_SIZE = 128
PIECE = 64
NEG = -1e30
MESH = pl.DeviceIdType.MESH
NT = (((1,), (1,)), ((), ()))
TN = (((0,), (0,)), ((), ()))
VMEM_LIMIT = 56 * 1024 * 1024


def ring_place(index, n):
    odd = index % 2
    return (1 - odd) * (index // 2) + odd * (n - 1 - index // 2)


def ring_member(place, n):
    back = place // (n // 2)
    return (1 - back) * (2 * place) + back * (2 * (n - place) - 1)


def around(n):
    me = lax.axis_index("ctx")
    place = ring_place(me, n)

    def member(offset):
        return ring_member((place + offset + 2 * n) % n, n)

    return me, member


def fused_kernel(
    n,
    n_tp,
    chunk,
    lengths,
    plan,
    q_hbm,
    g_hbm,
    o_hbm,
    k_hbm,
    v_hbm,
    w_hbm,
    dq_ref,
    dk_ref,
    dv_ref,
    di_ref,
    q_wide,
    g_wide,
    o_wide,
    k_all,
    v_all,
    queries,
    grads,
    delta,
    bias,
    scores,
    top,
    inverse,
    dq_acc,
    k_part,
    v_part,
    value_grad,
    weight,
    term_recv,
    part_send,
    part_recv,
    load_sem,
    ag_send_sem,
    ag_recv_sem,
    term_send_sem,
    term_recv_sem,
    part_send_sem,
    part_recv_sem,
    w_sem,
):
    me, member = around(n)
    dp, tp = lax.axis_index("dp"), lax.axis_index("tp")
    other = 1 - dp
    right, left = member(1), member(-1)
    toks, kv_width = k_hbm.shape
    kv_heads = kv_width // HEAD_SIZE
    per_group = q_hbm.shape[1] // kv_width
    cols = per_group * toks
    half = w_hbm.shape[0]
    share = 2 * half // n_tp
    chunks = share // chunk
    long, short = n // 2, (n - 1) // 2
    low = jnp.bfloat16

    def aim(way):
        return {"ctx": right if way == 1 else left}

    barrier = pltpu.get_barrier_semaphore()
    for k in range(1, n):
        pl.semaphore_signal(barrier, inc=1, device_id={"ctx": (me + k) % n}, device_id_type=MESH)
    pl.semaphore_signal(barrier, inc=1, device_id={"dp": other}, device_id_type=MESH)
    for k in range(1, n_tp):
        pl.semaphore_signal(barrier, inc=1, device_id={"tp": (tp + k) % n_tp}, device_id_type=MESH)
    own_rows = pl.ds(pl.multiple_of(dp * half, half), half)
    loads = [
        pltpu.make_async_copy(source, target, load_sem.at[i])
        for i, (source, target) in enumerate(
            (
                (k_hbm, k_all.at[me]),
                (q_hbm, q_wide),
                (g_hbm, g_wide),
                (o_hbm, o_wide),
                (v_hbm, v_all.at[me]),
                (w_hbm, weight.at[own_rows]),
            )
        )
    ]
    for load in loads:
        load.start()
    pl.semaphore_wait(barrier, n - 1 + n_tp)
    sends = []
    gathers = {}

    def gather_step(tensor, way, step):
        source, target = ((k_hbm, k_all), (v_hbm, v_all))[tensor]
        row = 2 * tensor + (0 if way == 1 else 1)
        block = member(-way * step)
        if step > 0:
            gathers[row, step - 1].wait_recv()
        count = long if (tensor == 0) == (way == 1) else short
        if step >= count:
            return
        copy = pltpu.make_async_remote_copy(
            src_ref=source if step == 0 else target.at[block],
            dst_ref=target.at[block],
            send_sem=ag_send_sem.at[row, step],
            recv_sem=ag_recv_sem.at[row, step],
            device_id=aim(way),
            device_id_type=MESH,
        )
        copy.start()
        gathers[row, step] = copy
        sends.append(copy)

    for tensor in range(2):
        gather_step(tensor, 1, 0)
        gather_step(tensor, -1, 0)
    w_copy = pltpu.make_async_remote_copy(
        src_ref=w_hbm,
        dst_ref=weight.at[own_rows],
        send_sem=w_sem.at[0],
        recv_sem=w_sem.at[1],
        device_id={"dp": other},
        device_id_type=MESH,
    )
    w_copy.start()

    lane = lax.broadcasted_iota(jnp.int32, (1, toks), 1)
    row_pos = jnp.zeros((1, toks), jnp.int32)
    for piece in range(toks // PIECE):
        here = plan[me * (toks // PIECE) + piece] * PIECE + lane - piece * PIECE
        row_pos = jnp.where(lane // PIECE == piece, here, row_pos)
    start = jnp.zeros((1, toks), jnp.int32)
    end = jnp.int32(0)
    for doc in range(lengths.shape[0]):
        end = end + lengths[doc]
        start = jnp.where(row_pos >= end, end, start)

    def fill(slot, carry):
        key_pos = plan[slot] * PIECE + lax.broadcasted_iota(jnp.int32, (PIECE, toks), 0)
        allowed = (key_pos >= start) & (key_pos <= row_pos)
        bias[pl.ds(pl.multiple_of(slot * PIECE, PIECE), PIECE), :] = jnp.where(allowed, 0.0, NEG)
        return carry

    lax.fori_loop(0, n * toks // PIECE, fill, 0)

    def head_span(h):
        return pl.ds(h * HEAD_SIZE, HEAD_SIZE)

    scale = HEAD_SIZE**-0.5 * math.log2(math.e)

    def score_block(block, first):
        rows = pl.ds(pl.multiple_of(block * toks, toks), toks)
        mask = jnp.concatenate([bias[rows, :]] * per_group, axis=1)
        for g in range(kv_heads):
            raw = lax.dot_general(
                k_all[block, :, head_span(g)], queries[g], NT, preferred_element_type=jnp.float32
            )
            part = raw * scale + mask
            scores[g, rows, :] = part
            high = jnp.max(part.reshape(toks // 8, 8, cols), axis=0)
            top[g] = high if first else jnp.maximum(top[g], high)

    loads[1].wait()
    for g in range(kv_heads):
        for h in range(per_group):
            queries[g, h * toks : (h + 1) * toks, :] = q_wide[:, head_span(g * per_group + h)]
    loads[0].wait()
    score_block(me, True)
    loads[2].wait()
    loads[3].wait()

    def prepare(g):
        for h in range(per_group):
            span = head_span(g * per_group + h)
            grads[g, h * toks : (h + 1) * toks, :] = g_wide[:, span]
            term = g_wide[:, span].astype(jnp.float32) * o_wide[:, span].astype(jnp.float32)
            delta[g, :, h * toks : (h + 1) * toks] = jnp.sum(term.T, axis=0, keepdims=True)

    todo = list(range(kv_heads))
    for step in range(1, long + 1):
        gather_step(0, 1, step)
        if step <= short:
            gather_step(0, -1, step)
            gather_step(1, 1, step)
        gather_step(1, -1, step)
        if todo:
            prepare(todo.pop(0))
        score_block(member(-step), False)
        if step <= short:
            score_block(member(step), False)
    for g in todo:
        prepare(g)
    terms = {}

    def scatter(tensor, g):
        part = v_part if tensor else k_part
        for k in range(1, n):
            peer = (me + k) % n
            copy = pltpu.make_async_remote_copy(
                src_ref=part.at[g, peer],
                dst_ref=term_recv.at[tensor, g, k - 1],
                send_sem=term_send_sem.at[tensor, g, k - 1],
                recv_sem=term_recv_sem.at[tensor, g, k - 1],
                device_id={"ctx": peer},
                device_id_type=MESH,
            )
            copy.start()
            terms[tensor, g, k] = copy
            sends.append(copy)

    def collect(tensor, g):
        block = (v_part if tensor else k_part)[g, me].astype(jnp.float32)
        for k in range(1, n):
            terms[tensor, g, k].wait_recv()
            block = block + term_recv[tensor, g, k - 1].astype(jnp.float32)
        block = block.astype(low)
        if tensor:
            dv_ref[:, head_span(g)] = block
            value_grad[:, head_span(g)] = block
        else:
            dk_ref[:, head_span(g)] = block

    for g in range(kv_heads):
        high = jnp.max(top[g], axis=0, keepdims=True)

        def expo(j, total):
            rows = pl.ds(pl.multiple_of(j * toks, toks), toks)
            part = jnp.exp2(scores[g, rows, :] - high)
            scores[g, rows, :] = part
            return total + jnp.sum(part.reshape(toks // 8, 8, cols), axis=0)

        total = lax.fori_loop(0, n, expo, jnp.zeros((8, cols), jnp.float32))
        inverse[g] = 1.0 / jnp.sum(total, axis=0, keepdims=True)
        def values_of(j, carry):
            rows = pl.ds(pl.multiple_of(j * toks, toks), toks)
            weights = scores[g, rows, :] * inverse[g]
            scores[g, rows, :] = weights
            v_part[g, j] = jnp.dot(
                weights.astype(low), grads[g], preferred_element_type=jnp.float32
            ).astype(low)
            return carry

        lax.fori_loop(0, n, values_of, 0)
        scatter(1, g)
    for load in loads[4:]:
        load.wait()

    def product(part, c):
        rows = pl.ds(pl.multiple_of(part * share + c * chunk, chunk), chunk)
        return lax.dot_general(
            value_grad[...], weight[rows, :], NT, preferred_element_type=jnp.float32
        ).astype(low)

    parts = {}

    def send_part(k, c):
        peer = (tp + k) % n_tp
        part_send[k - 1, c] = product(peer, c)
        copy = pltpu.make_async_remote_copy(
            src_ref=part_send.at[k - 1, c],
            dst_ref=part_recv.at[k - 1, c],
            send_sem=part_send_sem.at[k - 1, c],
            recv_sem=part_recv_sem.at[k - 1, c],
            device_id={"tp": peer},
            device_id_type=MESH,
        )
        copy.start()
        parts[k, c] = copy
        sends.append(copy)

    for g in range(kv_heads):
        if g == kv_heads - 1:
            for group in range(kv_heads):
                collect(1, group)
            w_copy.wait()
            for c in range(chunks):
                for k in range(1, n_tp):
                    send_part(k, c)

        def keys_of(j, carry):
            rows = pl.ds(pl.multiple_of(j * toks, toks), toks)
            grad_weights = lax.dot_general(
                v_all[j, :, head_span(g)], grads[g], NT, preferred_element_type=jnp.float32
            )
            grad_scores = (
                scores[g, rows, :] * ((grad_weights - delta[g]) * HEAD_SIZE**-0.5)
            ).astype(low)
            k_part[g, j] = jnp.dot(
                grad_scores, queries[g], preferred_element_type=jnp.float32
            ).astype(low)
            part = lax.dot_general(
                grad_scores, k_all[j, :, head_span(g)], TN, preferred_element_type=jnp.float32
            )
            dq_acc[...] += part
            return carry

        dq_acc[...] = jnp.zeros_like(dq_acc)
        lax.fori_loop(0, n, keys_of, 0)
        scatter(0, g)
        for h in range(per_group):
            dq_ref[:, head_span(g * per_group + h)] = dq_acc[h * toks : (h + 1) * toks].astype(low)
    for c in range(chunks):
        total = product(tp, c).astype(jnp.float32)
        for k in range(1, n_tp):
            parts[k, c].wait_recv()
            total = total + part_recv[k - 1, c].astype(jnp.float32)
        di_ref[:, c * chunk : (c + 1) * chunk] = total.astype(low)
    for g in range(kv_heads):
        collect(0, g)
    for copy in sends:
        copy.wait_send()


def solution(mesh):
    n, n_tp = mesh.shape["ctx"], mesh.shape["tp"]

    def on_device(lengths, plan, queries, keys, values, grads, outputs, weight):
        toks, kv_width = keys.shape[1:]
        q_width = queries.shape[2]
        kv_heads = kv_width // HEAD_SIZE
        cols = q_width // kv_width * toks
        half = weight.shape[0]
        share = 2 * half // n_tp
        chunk = 512
        chunks = share // chunk
        steps = n // 2
        low, wide = jnp.bfloat16, jnp.float32
        vmem = pl.BlockSpec(memory_space=pltpu.VMEM)
        smem = pl.BlockSpec(memory_space=pltpu.SMEM)
        hbm = pl.BlockSpec(memory_space=pl.ANY)
        narrow = jax.ShapeDtypeStruct((toks, kv_width), low)
        dma = pltpu.SemaphoreType.DMA
        query_grad, key_grad, value_grad, input_grad = pl.pallas_call(
            functools.partial(fused_kernel, n, n_tp, chunk),
            out_shape=(
                jax.ShapeDtypeStruct((toks, q_width), low),
                narrow,
                narrow,
                jax.ShapeDtypeStruct((toks, share), low),
            ),
            in_specs=[smem] * 2 + [hbm] * 6,
            out_specs=[vmem] * 4,
            scratch_shapes=[
                pltpu.VMEM((toks, q_width), low),
                pltpu.VMEM((toks, q_width), low),
                pltpu.VMEM((toks, q_width), low),
                pltpu.VMEM((n, toks, kv_width), low),
                pltpu.VMEM((n, toks, kv_width), low),
                pltpu.VMEM((kv_heads, cols, HEAD_SIZE), low),
                pltpu.VMEM((kv_heads, cols, HEAD_SIZE), low),
                pltpu.VMEM((kv_heads, 1, cols), wide),
                pltpu.VMEM((n * toks, toks), wide),
                pltpu.VMEM((kv_heads, n * toks, cols), wide),
                pltpu.VMEM((kv_heads, 8, cols), wide),
                pltpu.VMEM((kv_heads, 1, cols), wide),
                pltpu.VMEM((cols, HEAD_SIZE), wide),
                pltpu.VMEM((kv_heads, n, toks, HEAD_SIZE), low),
                pltpu.VMEM((kv_heads, n, toks, HEAD_SIZE), low),
                pltpu.VMEM((toks, kv_width), low),
                pltpu.VMEM((2 * half, kv_width), low),
                pltpu.VMEM((2, kv_heads, n - 1, toks, HEAD_SIZE), low),
                pltpu.VMEM((n_tp - 1, chunks, toks, chunk), low),
                pltpu.VMEM((n_tp - 1, chunks, toks, chunk), low),
                dma((6,)),
                dma((4, steps)),
                dma((4, steps)),
                dma((2, kv_heads, n - 1)),
                dma((2, kv_heads, n - 1)),
                dma((n_tp - 1, chunks)),
                dma((n_tp - 1, chunks)),
                dma((2,)),
            ],
            compiler_params=pltpu.CompilerParams(
                collective_id=0, has_side_effects=True, vmem_limit_bytes=VMEM_LIMIT
            ),
            name="fused_backward",
        )(lengths[0], plan[0], queries[0], grads[0], outputs[0], keys[0], values[0], weight)
        return query_grad[None], key_grad[None], value_grad[None], input_grad[None]

    spread = P("dp", "ctx", "tp")
    return jax.shard_map(
        on_device,
        mesh=mesh,
        in_specs=(P("dp", None), P("dp", None)) + (spread,) * 5 + (P("dp", "tp"),),
        out_specs=(spread,) * 4,
        check_vma=False,
    )
```

```python
import functools
import math

import jax
import jax.numpy as jnp
from jax import lax
from jax.experimental import pallas as pl
from jax.experimental.pallas import tpu as pltpu
from jax.sharding import PartitionSpec as P

QUERY_HEADS = 64
KEY_VALUE_HEADS = 8
HEAD_SIZE = 128
PIECE = 64
NEG = -1e30
MESH = pl.DeviceIdType.MESH
NT = (((1,), (1,)), ((), ()))
TN = (((0,), (0,)), ((), ()))
VMEM_LIMIT = 56 * 1024 * 1024


def ring_place(index, n):
    odd = index % 2
    return (1 - odd) * (index // 2) + odd * (n - 1 - index // 2)


def ring_member(place, n):
    back = place // (n // 2)
    return (1 - back) * (2 * place) + back * (2 * (n - place) - 1)


def around(n):
    me = lax.axis_index("ctx")
    place = ring_place(me, n)

    def member(offset):
        return ring_member((place + offset + 2 * n) % n, n)

    return me, member


def fused_kernel(
    n,
    n_tp,
    chunk,
    lengths,
    plan,
    q_hbm,
    g_hbm,
    o_hbm,
    k_hbm,
    v_hbm,
    w_hbm,
    dq_ref,
    dk_ref,
    dv_ref,
    di_ref,
    q_wide,
    g_wide,
    o_wide,
    k_all,
    v_all,
    queries,
    grads,
    delta,
    bias,
    scores,
    top,
    inverse,
    dq_acc,
    k_part,
    v_part,
    value_grad,
    weight,
    term_recv,
    part_send,
    part_recv,
    load_sem,
    ag_send_sem,
    ag_recv_sem,
    term_send_sem,
    term_recv_sem,
    part_send_sem,
    part_recv_sem,
    w_sem,
):
    me, member = around(n)
    dp, tp = lax.axis_index("dp"), lax.axis_index("tp")
    other = 1 - dp
    right, left = member(1), member(-1)
    toks, kv_width = k_hbm.shape
    kv_heads = kv_width // HEAD_SIZE
    per_group = q_hbm.shape[1] // kv_width
    cols = per_group * toks
    half = w_hbm.shape[0]
    share = 2 * half // n_tp
    chunks = share // chunk
    long, short = n // 2, (n - 1) // 2
    low = jnp.bfloat16

    def aim(way):
        return {"ctx": right if way == 1 else left}

    barrier = pltpu.get_barrier_semaphore()
    for k in range(1, n):
        pl.semaphore_signal(barrier, inc=1, device_id={"ctx": (me + k) % n}, device_id_type=MESH)
    pl.semaphore_signal(barrier, inc=1, device_id={"dp": other}, device_id_type=MESH)
    for k in range(1, n_tp):
        pl.semaphore_signal(barrier, inc=1, device_id={"tp": (tp + k) % n_tp}, device_id_type=MESH)
    own_rows = pl.ds(pl.multiple_of(dp * half, half), half)
    loads = [
        pltpu.make_async_copy(source, target, load_sem.at[i])
        for i, (source, target) in enumerate(
            (
                (k_hbm, k_all.at[me]),
                (q_hbm, q_wide),
                (g_hbm, g_wide),
                (o_hbm, o_wide),
                (v_hbm, v_all.at[me]),
                (w_hbm, weight.at[own_rows]),
            )
        )
    ]
    for load in loads:
        load.start()
    pl.semaphore_wait(barrier, n - 1 + n_tp)
    sends = []
    gathers = {}

    def gather_step(tensor, way, step):
        source, target = ((k_hbm, k_all), (v_hbm, v_all))[tensor]
        row = 2 * tensor + (0 if way == 1 else 1)
        block = member(-way * step)
        if step > 0:
            gathers[row, step - 1].wait_recv()
        count = long if (tensor == 0) == (way == 1) else short
        if step >= count:
            return
        copy = pltpu.make_async_remote_copy(
            src_ref=source if step == 0 else target.at[block],
            dst_ref=target.at[block],
            send_sem=ag_send_sem.at[row, step],
            recv_sem=ag_recv_sem.at[row, step],
            device_id=aim(way),
            device_id_type=MESH,
        )
        copy.start()
        gathers[row, step] = copy
        sends.append(copy)

    for tensor in range(2):
        gather_step(tensor, 1, 0)
        gather_step(tensor, -1, 0)
    w_copy = pltpu.make_async_remote_copy(
        src_ref=w_hbm,
        dst_ref=weight.at[own_rows],
        send_sem=w_sem.at[0],
        recv_sem=w_sem.at[1],
        device_id={"dp": other},
        device_id_type=MESH,
    )
    w_copy.start()

    lane = lax.broadcasted_iota(jnp.int32, (1, toks), 1)
    row_pos = jnp.zeros((1, toks), jnp.int32)
    for piece in range(toks // PIECE):
        here = plan[me * (toks // PIECE) + piece] * PIECE + lane - piece * PIECE
        row_pos = jnp.where(lane // PIECE == piece, here, row_pos)
    start = jnp.zeros((1, toks), jnp.int32)
    end = jnp.int32(0)
    for doc in range(lengths.shape[0]):
        end = end + lengths[doc]
        start = jnp.where(row_pos >= end, end, start)

    def fill(slot, carry):
        key_pos = plan[slot] * PIECE + lax.broadcasted_iota(jnp.int32, (PIECE, toks), 0)
        allowed = (key_pos >= start) & (key_pos <= row_pos)
        bias[pl.ds(pl.multiple_of(slot * PIECE, PIECE), PIECE), :] = jnp.where(allowed, 0.0, NEG)
        return carry

    lax.fori_loop(0, n * toks // PIECE, fill, 0)

    def head_span(h):
        return pl.ds(h * HEAD_SIZE, HEAD_SIZE)

    scale = HEAD_SIZE**-0.5 * math.log2(math.e)

    def score_block(block, first):
        rows = pl.ds(pl.multiple_of(block * toks, toks), toks)
        mask = jnp.concatenate([bias[rows, :]] * per_group, axis=1)
        for g in range(kv_heads):
            raw = lax.dot_general(
                k_all[block, :, head_span(g)], queries[g], NT, preferred_element_type=jnp.float32
            )
            part = raw * scale + mask
            scores[g, rows, :] = part
            high = jnp.max(part.reshape(toks // 8, 8, cols), axis=0)
            top[g] = high if first else jnp.maximum(top[g], high)

    loads[1].wait()
    for g in range(kv_heads):
        for h in range(per_group):
            queries[g, h * toks : (h + 1) * toks, :] = q_wide[:, head_span(g * per_group + h)]
    loads[0].wait()
    score_block(me, True)
    loads[2].wait()
    loads[3].wait()

    def prepare(g):
        for h in range(per_group):
            span = head_span(g * per_group + h)
            grads[g, h * toks : (h + 1) * toks, :] = g_wide[:, span]
            term = g_wide[:, span].astype(jnp.float32) * o_wide[:, span].astype(jnp.float32)
            delta[g, :, h * toks : (h + 1) * toks] = jnp.sum(term.T, axis=0, keepdims=True)

    todo = list(range(kv_heads))
    for step in range(1, long + 1):
        gather_step(0, 1, step)
        if step <= short:
            gather_step(0, -1, step)
            gather_step(1, 1, step)
        gather_step(1, -1, step)
        if todo:
            prepare(todo.pop(0))
        score_block(member(-step), False)
        if step <= short:
            score_block(member(step), False)
    for g in todo:
        prepare(g)
    terms = {}

    def scatter(tensor, g):
        part = v_part if tensor else k_part
        for k in range(1, n):
            peer = (me + k) % n
            copy = pltpu.make_async_remote_copy(
                src_ref=part.at[g, peer],
                dst_ref=term_recv.at[tensor, g, k - 1],
                send_sem=term_send_sem.at[tensor, g, k - 1],
                recv_sem=term_recv_sem.at[tensor, g, k - 1],
                device_id={"ctx": peer},
                device_id_type=MESH,
            )
            copy.start()
            terms[tensor, g, k] = copy
            sends.append(copy)

    def collect(tensor, g):
        block = (v_part if tensor else k_part)[g, me].astype(jnp.float32)
        for k in range(1, n):
            terms[tensor, g, k].wait_recv()
            block = block + term_recv[tensor, g, k - 1].astype(jnp.float32)
        block = block.astype(low)
        if tensor:
            dv_ref[:, head_span(g)] = block
            value_grad[:, head_span(g)] = block
        else:
            dk_ref[:, head_span(g)] = block

    for g in range(kv_heads):
        high = jnp.max(top[g], axis=0, keepdims=True)

        def expo(j, total):
            rows = pl.ds(pl.multiple_of(j * toks, toks), toks)
            part = jnp.exp2(scores[g, rows, :] - high)
            scores[g, rows, :] = part
            return total + jnp.sum(part.reshape(toks // 8, 8, cols), axis=0)

        total = lax.fori_loop(0, n, expo, jnp.zeros((8, cols), jnp.float32))
        inverse[g] = 1.0 / jnp.sum(total, axis=0, keepdims=True)
        def values_of(j, carry):
            rows = pl.ds(pl.multiple_of(j * toks, toks), toks)
            weights = scores[g, rows, :] * inverse[g]
            scores[g, rows, :] = weights
            v_part[g, j] = jnp.dot(
                weights.astype(low), grads[g], preferred_element_type=jnp.float32
            ).astype(low)
            return carry

        lax.fori_loop(0, n, values_of, 0)
        scatter(1, g)
    for load in loads[4:]:
        load.wait()

    def product(part, c):
        rows = pl.ds(pl.multiple_of(part * share + c * chunk, chunk), chunk)
        return lax.dot_general(
            value_grad[...], weight[rows, :], NT, preferred_element_type=jnp.float32
        ).astype(low)

    parts = {}

    def send_part(k, c):
        peer = (tp + k) % n_tp
        part_send[k - 1, c] = product(peer, c)
        copy = pltpu.make_async_remote_copy(
            src_ref=part_send.at[k - 1, c],
            dst_ref=part_recv.at[k - 1, c],
            send_sem=part_send_sem.at[k - 1, c],
            recv_sem=part_recv_sem.at[k - 1, c],
            device_id={"tp": peer},
            device_id_type=MESH,
        )
        copy.start()
        parts[k, c] = copy
        sends.append(copy)

    for g in range(kv_heads):
        if g == kv_heads - 1:
            for group in range(kv_heads):
                collect(1, group)
            w_copy.wait()
            for c in range(chunks):
                for k in range(1, n_tp):
                    send_part(k, c)

        def keys_of(j, carry):
            rows = pl.ds(pl.multiple_of(j * toks, toks), toks)
            grad_weights = lax.dot_general(
                v_all[j, :, head_span(g)], grads[g], NT, preferred_element_type=jnp.float32
            )
            grad_scores = (
                scores[g, rows, :] * ((grad_weights - delta[g]) * HEAD_SIZE**-0.5)
            ).astype(low)
            k_part[g, j] = jnp.dot(
                grad_scores, queries[g], preferred_element_type=jnp.float32
            ).astype(low)
            part = lax.dot_general(
                grad_scores, k_all[j, :, head_span(g)], TN, preferred_element_type=jnp.float32
            )
            dq_acc[...] += part
            return carry

        dq_acc[...] = jnp.zeros_like(dq_acc)
        lax.fori_loop(0, n, keys_of, 0)
        scatter(0, g)
        for h in range(per_group):
            dq_ref[:, head_span(g * per_group + h)] = dq_acc[h * toks : (h + 1) * toks].astype(low)
    for c in range(chunks):
        total = product(tp, c).astype(jnp.float32)
        for k in range(1, n_tp):
            parts[k, c].wait_recv()
            total = total + part_recv[k - 1, c].astype(jnp.float32)
        di_ref[:, c * chunk : (c + 1) * chunk] = total.astype(low)
    for g in range(kv_heads):
        collect(0, g)
    for copy in sends:
        copy.wait_send()


def place_kernel(*refs):
    count = len(refs) // 2
    copies = [
        pltpu.make_async_copy(refs[i], refs[count + i], refs[-1].at[i]) for i in range(count)
    ]
    for copy in copies:
        copy.start()
    for copy in copies:
        copy.wait()


def place(arrays):
    hbm = pl.BlockSpec(memory_space=pl.ANY)
    return pl.pallas_call(
        place_kernel,
        out_shape=tuple(jax.ShapeDtypeStruct(a.shape, a.dtype) for a in arrays),
        in_specs=[hbm] * len(arrays),
        out_specs=[hbm] * len(arrays),
        scratch_shapes=[pltpu.SemaphoreType.DMA((len(arrays),))],
        name="place_results",
    )(*arrays)


def solution(mesh):
    n, n_tp = mesh.shape["ctx"], mesh.shape["tp"]

    def on_device(lengths, plan, queries, keys, values, grads, outputs, weight):
        toks, kv_width = keys.shape[1:]
        q_width = queries.shape[2]
        kv_heads = kv_width // HEAD_SIZE
        cols = q_width // kv_width * toks
        half = weight.shape[0]
        share = 2 * half // n_tp
        chunk = 512
        chunks = share // chunk
        steps = n // 2
        low, wide = jnp.bfloat16, jnp.float32
        vmem = pl.BlockSpec(memory_space=pltpu.VMEM)
        smem = pl.BlockSpec(memory_space=pltpu.SMEM)
        hbm = pl.BlockSpec(memory_space=pl.ANY)
        narrow = jax.ShapeDtypeStruct((toks, kv_width), low)
        dma = pltpu.SemaphoreType.DMA
        query_grad, key_grad, value_grad, input_grad = pl.pallas_call(
            functools.partial(fused_kernel, n, n_tp, chunk),
            out_shape=(
                jax.ShapeDtypeStruct((toks, q_width), low),
                narrow,
                narrow,
                jax.ShapeDtypeStruct((toks, share), low),
            ),
            in_specs=[smem] * 2 + [hbm] * 6,
            out_specs=[vmem] * 4,
            scratch_shapes=[
                pltpu.VMEM((toks, q_width), low),
                pltpu.VMEM((toks, q_width), low),
                pltpu.VMEM((toks, q_width), low),
                pltpu.VMEM((n, toks, kv_width), low),
                pltpu.VMEM((n, toks, kv_width), low),
                pltpu.VMEM((kv_heads, cols, HEAD_SIZE), low),
                pltpu.VMEM((kv_heads, cols, HEAD_SIZE), low),
                pltpu.VMEM((kv_heads, 1, cols), wide),
                pltpu.VMEM((n * toks, toks), wide),
                pltpu.VMEM((kv_heads, n * toks, cols), wide),
                pltpu.VMEM((kv_heads, 8, cols), wide),
                pltpu.VMEM((kv_heads, 1, cols), wide),
                pltpu.VMEM((cols, HEAD_SIZE), wide),
                pltpu.VMEM((kv_heads, n, toks, HEAD_SIZE), low),
                pltpu.VMEM((kv_heads, n, toks, HEAD_SIZE), low),
                pltpu.VMEM((toks, kv_width), low),
                pltpu.VMEM((2 * half, kv_width), low),
                pltpu.VMEM((2, kv_heads, n - 1, toks, HEAD_SIZE), low),
                pltpu.VMEM((n_tp - 1, chunks, toks, chunk), low),
                pltpu.VMEM((n_tp - 1, chunks, toks, chunk), low),
                dma((6,)),
                dma((4, steps)),
                dma((4, steps)),
                dma((2, kv_heads, n - 1)),
                dma((2, kv_heads, n - 1)),
                dma((n_tp - 1, chunks)),
                dma((n_tp - 1, chunks)),
                dma((2,)),
            ],
            compiler_params=pltpu.CompilerParams(
                collective_id=0, has_side_effects=True, vmem_limit_bytes=VMEM_LIMIT
            ),
            name="fused_backward",
        )(lengths[0], plan[0], queries[0], grads[0], outputs[0], keys[0], values[0], weight)
        query_grad, key_grad, value_grad, input_grad = place(
            (query_grad, key_grad, value_grad, input_grad)
        )
        return query_grad[None], key_grad[None], value_grad[None], input_grad[None]

    spread = P("dp", "ctx", "tp")
    return jax.shard_map(
        on_device,
        mesh=mesh,
        in_specs=(P("dp", None), P("dp", None)) + (spread,) * 5 + (P("dp", "tp"),),
        out_specs=(spread,) * 4,
        check_vma=False,
    )
```
